32 devices in a mesh: grp: 2 (over y), gx: 4 (over z), gy: 2 (over x), gz: 2 (over core).
Axes of the slice: x: 2, y: 2, z: 4, core: 2. Of those that a mesh axis runs over, the one named last changes fastest.
Arguments:
- core_tensor: float32 [6, 256, 256, 256], P('grp', 'gz', 'gx', 'gy'), parts along dimension 0, may hold values from -6 to 6
- factor_x: float32 [512, 512], P('gx', 'grp'), parts along dimension 1, may hold values from -0.375 to 0.375
- factor_y: float32 [512, 512], P('gy', 'grp'), parts along dimension 1, may hold values from -0.375 to 0.375
- factor_z: float32 [32, 256], P('grp', 'gz'), parts along dimension 0, may hold values from -0.375 to 0.375
- suspect_voxel_list: int32 [16, 1024], P(('gx', 'gy', 'gz'), 'grp'), parts along dimension 1, may hold values from 0 to 262143
Outputs:
- velocity: float32 [6, 16, 512, 512], P('grp', 'gz', 'gx', 'gy'), parts along dimension 0
- invariants: float32 [8, 8192], P('grp', ('gx', 'gy', 'gz')), parts along dimension 0
The draws below stay inside these ranges and needn't reach their ends.
There are 2 independent parts, one for each index of `grp`. The reference program is written for one: setup_inputs(seed, part) draws one part's arguments, and reference() takes and returns one part's arrays. A program takes and returns all parts, laid end to end along the dimension named above; each array names one. Nothing has to cross between parts.
Inputs may be any that keep to these rules, and one draw needn't show every extreme that they name: `suspect_voxel_list`: entries may repeat within a brick's list.
All inputs are finite; a program needn't handle non-finite values.
Results may differ from the reference program's by a relative error of at most 0.0003.
Values sent between devices are 32-bit elements; how exact they have to be, the bound alone decides.
A program may use at most 64 MiB of HBM per device.

```python
import jax
import jax.numpy as jnp
from jax import lax

R1 = 256
R2 = 256
R3 = 256
CX = 128
CY = 256
CZ = 8
NCAND = 512
NX = 512
NY = 512
NZ = 16
BRICKS = 16
N_GX = 4
N_GY = 2
N_GZ = 2


def place_ends(result, key, least, high):
    longest = result.shape.index(max(result.shape))
    spots = []
    for shift in (0, 1):
        where = [jax.random.randint(jax.random.fold_in(key, axis), (), 0, length) for axis, length in enumerate(result.shape)]
        where[longest] = (where[longest] + shift) % result.shape[longest]
        spots.append(tuple(where))
    return result.at[spots[0]].set(least).at[spots[1]].set(high)


def steps_of(own_key, shape, cuts, least, largest):
    def one(position, shards_of):
        heights = jax.random.uniform(jax.random.fold_in(jax.random.fold_in(own_key, 6), position), (shards_of,), jnp.float32, least / len(cuts), largest / len(cuts))
        return jnp.repeat(jnp.exp(heights), shape[position] // shards_of).reshape((-1,) + (1,) * (len(shape) - position - 1))

    gain = one(*cuts[0])
    for cut in cuts[1:]:
        gain = gain * one(*cut)
    return gain


def normal_values(rng, dims, deviation, bound, pieces=(), kind=jnp.bfloat16):
    factor_of = steps_of(rng, dims, pieces, -0.22, 0.18) if pieces else 1.0
    array = jax.random.normal(rng, dims, jnp.float32) * deviation * factor_of
    return jnp.minimum(jnp.maximum(array, -bound), bound).astype(kind)


def setup_inputs(seed: int = 0, part: int = 0) -> dict:
    arg_keys = jax.random.split(jax.random.key(seed), 6)
    part_splits = jax.random.split(jax.random.fold_in(arg_keys[5], part), 6)
    core_tensor = normal_values(part_splits[0], (3, R3, R1, R2), 1.0, 6.0, ((1, 2), (2, 4), (3, 2)), jnp.float32)
    factor_x = normal_values(part_splits[1], (NX, R1), R1 ** -0.5, 0.375, ((0, 4),), jnp.float32)
    factor_y = normal_values(part_splits[2], (NY, R2), R2 ** -0.5, 0.375, ((0, 2),), jnp.float32)
    factor_z = normal_values(part_splits[3], (NZ, R3), R3 ** -0.5, 0.375, ((1, 2),), jnp.float32)
    suspect_voxel_list = place_ends(jax.random.randint(part_splits[4], (BRICKS, NCAND), 0, CZ * CX * CY), jax.random.fold_in(part_splits[4], 1), 0, (CZ * CX * CY) - 1).astype(jnp.int32)
    return dict(core_tensor=core_tensor, factor_x=factor_x, factor_y=factor_y, factor_z=factor_z, suspect_voxel_list=suspect_voxel_list)


highest = lax.Precision.HIGHEST


def gradient_invariants(grad_x, grad_y, grad_z):
    jacobian = [[grad_x[0], grad_y[0], grad_z[0]], [grad_x[1], grad_y[1], grad_z[1]], [grad_x[2], grad_y[2], grad_z[2]]]
    jacobian_trace_p = -(jacobian[0][0] + jacobian[1][1] + jacobian[2][2])
    square_trace = jacobian[0][0] * jacobian[0][0]
    for first in range(3):
        for second in range(3):
            if first + second > 0:
                square_trace = square_trace + jacobian[first][second] * jacobian[second][first]
    jacobian_minor_q = 0.5 * (jacobian_trace_p * jacobian_trace_p - square_trace)
    determinant = (jacobian[0][0] * (jacobian[1][1] * jacobian[2][2] - jacobian[1][2] * jacobian[2][1])
                   - jacobian[0][1] * (jacobian[1][0] * jacobian[2][2] - jacobian[1][2] * jacobian[2][0])
                   + jacobian[0][2] * (jacobian[1][0] * jacobian[2][1] - jacobian[1][1] * jacobian[2][0]))
    jacobian_volume_r = -determinant
    eigen_sort_test = jacobian_minor_q * jacobian_minor_q * jacobian_minor_q + 6.75 * jacobian_volume_r * jacobian_volume_r
    return jnp.stack([jacobian_trace_p, jacobian_minor_q, jacobian_volume_r, eigen_sort_test])


def reference(core_tensor, factor_x, factor_y, factor_z, suspect_voxel_list):
    slab_sum = jnp.einsum('kg,cgab->ckab', factor_z, core_tensor, precision=highest)
    middle = jnp.einsum('ia,ckab->ckib', factor_x, slab_sum, precision=highest)
    velocity = jnp.einsum('jb,ckib->ckij', factor_y, middle, precision=highest)
    padded = jnp.pad(velocity, ((0, 0), (1, 1), (1, 1), (1, 1)))
    unrolled_vector = padded.reshape(3, -1)
    bricks = jnp.arange(N_GX * N_GY * N_GZ, dtype=jnp.int32)
    brick_x = bricks // (N_GY * N_GZ)
    brick_y = (bricks // N_GZ) % N_GY
    brick_z = bricks % N_GZ
    plane = suspect_voxel_list // (CX * CY)
    row_x = (suspect_voxel_list // CY) % CX
    col_y = suspect_voxel_list % CY
    glob_z = brick_z[:, None] * CZ + plane + 1
    glob_x = brick_x[:, None] * CX + row_x + 1
    glob_y = brick_y[:, None] * CY + col_y + 1
    y_step_length = NY + 2
    stride_z = (NX + 2) * (NY + 2)
    centre = (glob_z * stride_z + glob_x * y_step_length + glob_y).reshape(-1).astype(jnp.int32)

    def sample_at(offset):
        return jnp.take(unrolled_vector, centre + offset, axis=1)

    grad_x = 0.5 * (sample_at(y_step_length) - sample_at(-y_step_length))
    grad_y = 0.5 * (sample_at(1) - sample_at(-1))
    grad_z = 0.5 * (sample_at(stride_z) - sample_at(-stride_z))
    return velocity, gradient_invariants(grad_x, grad_y, grad_z)
```

```python
import functools

import jax
import jax.numpy as jnp
from jax import lax
from jax.experimental import pallas as pl
from jax.experimental.pallas import tpu as pltpu
from jax.sharding import PartitionSpec as P

MESH = pl.DeviceIdType.MESH
F32 = jnp.float32
BF16 = jnp.bfloat16
SUB = 8
HALVES = 2


def split(value):
    high = value.astype(BF16)
    return high, (value - high.astype(F32)).astype(BF16)


def dot(left, right):
    return jnp.dot(left, right, preferred_element_type=F32)


def dot_last(left, right):
    return lax.dot_general(left, right, (((1,), (1,)), ((), ())), preferred_element_type=F32)


def exchange_kernel(
    sizes, core_hbm, fx_ref, fy_ref, fz_ref, wide_ref, fy_halo_ref,
    core_ref, part_ref, pair_ref, slab_ref, fx_halo_ref, kron_ref, fx_ref2,
    core_sem, pair_send, pair_recv, right_send, left_send, slab_recv,
    y_send, y_recv, z_send, z_recv, edge_send, edge_recv,
):
    nx, ny, nz = sizes
    comps, ranks_z, ranks_a, ranks_b = core_ref.shape
    planes = part_ref.shape[1]
    own = planes // nz
    chunk = own // HALVES
    cells_x = fx_ref.shape[0]
    rows = wide_ref.shape[3]
    px = lax.axis_index("gx")
    py = lax.axis_index("gy")
    pz = lax.axis_index("gz")

    for c in range(comps):
        pltpu.make_async_copy(core_hbm.at[c], core_ref.at[c], core_sem.at[c]).start()

    fx_halo_ref[...] = jnp.zeros_like(fx_halo_ref)
    fy_halo_ref[...] = jnp.zeros_like(fy_halo_ref)
    wide_ref[:, :, pl.ds(own + 1 - pz, 1)] = jnp.zeros(
        (ny, comps, 1, rows, ranks_b), F32
    )

    has_left, has_right = px > 0, px < nx - 1
    below, above = py > 0, py < ny - 1
    partner = {"gz": 1 - pz}
    barrier = pltpu.get_barrier_semaphore()

    @pl.when(has_left)
    def _():
        pl.semaphore_signal(barrier, inc=1, device_id={"gx": px - 1}, device_id_type=MESH)

    @pl.when(has_right)
    def _():
        pl.semaphore_signal(barrier, inc=1, device_id={"gx": px + 1}, device_id_type=MESH)

    for step in range(1, ny):
        pl.semaphore_signal(
            barrier, inc=1, device_id={"gy": lax.rem(py + step, ny)}, device_id_type=MESH
        )
    pl.semaphore_signal(barrier, inc=1, device_id=partner, device_id_type=MESH)

    zh, zl = split(fz_ref[...])
    tall = planes * SUB
    wide = ranks_z * SUB
    spread = (
        lax.broadcasted_iota(jnp.int32, (tall, planes), 0) // SUB
        == lax.broadcasted_iota(jnp.int32, (tall, planes), 1)
    ).astype(F32).astype(BF16)
    repeat = (
        lax.broadcasted_iota(jnp.int32, (ranks_z, wide), 1) // SUB
        == lax.broadcasted_iota(jnp.int32, (ranks_z, wide), 0)
    ).astype(F32).astype(BF16)
    same = (
        lax.broadcasted_iota(jnp.int32, (tall, wide), 0) % SUB
        == lax.broadcasted_iota(jnp.int32, (tall, wide), 1) % SUB
    )
    for index, piece in enumerate((zh, zl)):
        grown = dot(dot(spread, piece).astype(BF16), repeat)
        kron_ref[index * tall : (index + 1) * tall] = jnp.where(same, grown, 0.0).astype(BF16)

    greeted = has_left.astype(jnp.int32) + has_right.astype(jnp.int32) + ny
    pl.semaphore_wait(barrier, greeted)

    edges = []
    for index, (axis, at, low, high, source, target) in enumerate((
        ("gx", px, has_left, has_right, fx_ref, fx_halo_ref),
        ("gy", py, below, above, fy_ref, fy_halo_ref),
    )):
        last = source.shape[0] - SUB
        up = pltpu.make_async_remote_copy(
            source.at[pl.ds(last, SUB)], target.at[0], edge_send.at[index, 0],
            edge_recv.at[index, 0], device_id={axis: at + 1}, device_id_type=MESH,
        )
        down = pltpu.make_async_remote_copy(
            source.at[pl.ds(0, SUB)], target.at[1], edge_send.at[index, 1],
            edge_recv.at[index, 1], device_id={axis: at - 1}, device_id_type=MESH,
        )
        pl.when(high)(up.start)
        pl.when(low)(down.start)
        edges.append((low, high, up, down))

    def pair_copy(c):
        return pltpu.make_async_remote_copy(
            part_ref.at[c, pl.ds((1 - pz) * own, own)], pair_ref.at[c], pair_send.at[c],
            pair_recv.at[c], device_id=partner, device_id_type=MESH,
        )

    def slab_copy(q, origin, sem, target):
        return pltpu.make_async_remote_copy(
            slab_ref.at[q, origin], slab_ref.at[q, origin], sem.at[q, origin],
            slab_recv.at[q, origin], device_id={"gx": target}, device_id_type=MESH,
        )

    def contract_z(c):
        pltpu.make_async_copy(core_hbm.at[c], core_ref.at[c], core_sem.at[c]).wait()

        def body(step, carry):
            first = pl.multiple_of(step * 2 * SUB, SUB)
            both = jnp.concatenate(
                [
                    core_ref[c, :, pl.ds(first + at, SUB), :].reshape(wide, ranks_b)
                    for at in (0, SUB)
                ],
                axis=1,
            )
            high, low = split(both)
            stacked = dot(kron_ref[...], high)
            out = stacked[:tall] + stacked[tall:] + dot(kron_ref[:tall], low)
            for index, at in enumerate((0, SUB)):
                part_ref[c, :, pl.ds(first + at, SUB), :] = out[
                    :, index * ranks_b : (index + 1) * ranks_b
                ].reshape(planes, SUB, ranks_b)
            return carry

        lax.fori_loop(0, ranks_a // (2 * SUB), body, 0)
        pair_copy(c).start()

    def finish_z(c):
        pair_copy(c).wait_recv()
        for half in range(HALVES):
            q = c * HALVES + half
            slab_ref[q, px] = (
                part_ref[c, pl.ds(pz * own + half * chunk, chunk)]
                + pair_ref[c, half * chunk : (half + 1) * chunk]
            )

            @pl.when(has_right)
            def _():
                slab_copy(q, px, right_send, px + 1).start()

            @pl.when(has_left)
            def _():
                slab_copy(q, px, left_send, px - 1).start()

    contract_z(0)
    for c in range(1, comps):
        contract_z(c)
        finish_z(c - 1)
    finish_z(comps - 1)

    for low, high, up, down in edges:
        pl.when(low)(up.wait_recv)
        pl.when(high)(down.wait_recv)
    tile = lax.broadcasted_iota(jnp.int32, (2 * SUB, fx_ref.shape[1]), 0)
    outer = jnp.where(
        tile == 0, fx_halo_ref[0, SUB - 1 : SUB, :],
        jnp.where(tile == 1, fx_halo_ref[1, 0:1, :], 0.0),
    )
    full = cells_x + 2 * SUB
    xh, xl = split(jnp.concatenate([fx_ref[...], outer], axis=0))
    fx_ref2[:full] = xh
    fx_ref2[full:] = xl

    def y_copy(q, step):
        c, half = q // HALVES, q % HALVES
        block = wide_ref.at[py, c, pl.ds(half * chunk, chunk)]
        return pltpu.make_async_remote_copy(
            block, block, y_send.at[q, step - 1], y_recv.at[q, step - 1],
            device_id={"gy": lax.rem(py + step, ny)}, device_id_type=MESH,
        )

    def y_arrived(q, step):
        c, half = q // HALVES, q % HALVES
        block = wide_ref.at[lax.rem(py + ny - step, ny), c, pl.ds(half * chunk, chunk)]
        return pltpu.make_async_remote_copy(
            block, block, y_send.at[q, step - 1], y_recv.at[q, step - 1],
            device_id={"gy": lax.rem(py + step, ny)}, device_id_type=MESH,
        )

    def z_copy(c, step):
        owner = lax.rem(py + ny - step, ny)
        edge = (1 - pz) * (own - 1)
        return pltpu.make_async_remote_copy(
            wide_ref.at[owner, c, edge], wide_ref.at[owner, c, own + 1 - pz],
            z_send.at[c, step], z_recv.at[c, step], device_id=partner, device_id_type=MESH,
        )

    for q in range(comps * HALVES):
        c, half = q // HALVES, q % HALVES
        for hop in range(1, nx):
            @pl.when(px >= hop)
            def _():
                slab_copy(q, px - hop, right_send, px).wait_recv()

                @pl.when(has_right)
                def _():
                    slab_copy(q, px - hop, right_send, px + 1).start()

            @pl.when(px + hop < nx)
            def _():
                slab_copy(q, px + hop, left_send, px).wait_recv()

                @pl.when(has_left)
                def _():
                    slab_copy(q, px + hop, left_send, px - 1).start()

        for k in range(0, chunk, 2):
            both = jnp.concatenate(
                [slab_ref[q, :, k + at].reshape(nx * ranks_a, ranks_b) for at in (0, 1)], axis=1
            )
            high, low = split(both)
            stacked = dot(fx_ref2[...], high)
            out = stacked[:full] + stacked[full:] + dot(fx_ref2[:full], low)
            for at in (0, 1):
                wide_ref[py, c, half * chunk + k + at] = out[
                    :rows, at * ranks_b : (at + 1) * ranks_b
                ]
        for step in range(1, ny):
            y_copy(q, step).start()
        if half == HALVES - 1:
            z_copy(c, 0).start()

    for c in range(comps):
        for step in range(1, ny):
            for half in range(HALVES):
                y_arrived(c * HALVES + half, step).wait_recv()
            z_copy(c, step).start()

    for low, high, up, down in edges:
        pl.when(high)(up.wait_send)
        pl.when(low)(down.wait_send)
    for c in range(comps):
        pair_copy(c).wait_send()
    for q in range(comps * HALVES):
        for origin in range(nx):
            @pl.when((origin <= px) & has_right)
            def _():
                slab_copy(q, origin, right_send, px + 1).wait_send()

            @pl.when((origin >= px) & has_left)
            def _():
                slab_copy(q, origin, left_send, px - 1).wait_send()
        for step in range(1, ny):
            y_copy(q, step).wait_send()
    for c in range(comps):
        for step in range(ny):
            z_copy(c, step).wait_send()
            z_copy(c, step).wait_recv()


def field_kernel(
    cells_x, cells_y, wide_ref, fy_ref, fy_halo_ref, list_ref, field_ref, inv_ref,
    rows_ref, fy_rows_ref, prod_ref,
):
    ny, comps, slots, _, ranks_b = wide_ref.shape
    own = slots - 2
    ranks = ny * ranks_b
    lanes = 128
    parts = ranks // lanes
    count = list_ref.shape[1]
    per_plane = cells_x + 2

    def joined(c, k, start, size):
        return jnp.concatenate(
            [wide_ref[y, c, k, start : start + size, :] for y in range(ny)], axis=1
        )

    for c in range(comps):
        for k in range(slots):
            spot = 0 if k == own + 1 else k + 1
            base = spot * per_plane * SUB
            inner = joined(c, k, 0, cells_x)
            outer = joined(c, k, cells_x, SUB)
            for part in range(parts):
                cut = slice(part * lanes, (part + 1) * lanes)
                lane = c * parts + part
                rows_ref[pl.ds(base + SUB + lane, cells_x, stride=SUB), :] = inner[:, cut]
                rows_ref[pl.ds(base + lane, 1), :] = outer[0:1, cut]
                rows_ref[pl.ds(base + (cells_x + 1) * SUB + lane, 1), :] = outer[1:2, cut]
    for c in range(comps):
        for part in range(parts):
            cut = slice(part * lanes, (part + 1) * lanes)
            lane = c * parts + part
            fy_rows_ref[pl.ds(SUB + lane, cells_y, stride=SUB), :] = fy_ref[:, cut]
            fy_rows_ref[pl.ds(lane, 1), :] = fy_halo_ref[0, SUB - 1 : SUB, cut]
            fy_rows_ref[pl.ds((cells_y + 1) * SUB + lane, 1), :] = fy_halo_ref[1, 0:1, cut]

    def candidate(n, carry):
        cell = list_ref[0, n]
        plane = cell // (cells_x * cells_y)
        row = cell // cells_y % cells_x
        column = cell % cells_y
        spot = (plane + 1) * per_plane + row + 1

        def at(ref, index):
            return ref[pl.ds(pl.multiple_of(index * SUB, SUB), SUB), :]

        centre = at(fy_rows_ref, column + 1)
        here = pl.ds(pl.multiple_of(n * SUB, SUB), SUB)
        prod_ref[0, here, :] = (at(rows_ref, spot + 1) - at(rows_ref, spot - 1)) * centre
        prod_ref[1, here, :] = at(rows_ref, spot) * (
            at(fy_rows_ref, column + 2) - at(fy_rows_ref, column)
        )
        prod_ref[2, here, :] = (
            at(rows_ref, spot + per_plane) - at(rows_ref, spot - per_plane)
        ) * centre
        return carry

    lax.fori_loop(0, count, candidate, 0, unroll=8)

    fh, fl = split(fy_ref[...])
    for c in range(comps):
        flat = jnp.concatenate(
            [
                wide_ref[y, c, 0:own, 0:cells_x, :].reshape(own * cells_x, ranks_b)
                for y in range(ny)
            ],
            axis=1,
        )
        high, low = split(flat)
        out = dot_last(high, fh) + dot_last(high, fl) + dot_last(low, fh)
        field_ref[c] = out.reshape(own, cells_x, cells_y)

    ones = jnp.ones((SUB * 2, lanes), F32).astype(BF16)

    def grad(c, d):
        total = prod_ref[d, pl.ds(c * parts, count, stride=SUB), :]
        for part in range(1, parts):
            total = total + prod_ref[d, pl.ds(c * parts + part, count, stride=SUB), :]
        high, low = split(total)
        return 0.5 * (dot_last(ones, high) + dot_last(ones, low))[0:1, :]

    j = [[grad(c, d) for d in range(3)] for c in range(3)]
    p = -(j[0][0] + j[1][1] + j[2][2])
    square = j[0][0] * j[0][0]
    for a in range(3):
        for b in range(3):
            if a + b > 0:
                square = square + j[a][b] * j[b][a]
    q = 0.5 * (p * p - square)
    det = (
        j[0][0] * (j[1][1] * j[2][2] - j[1][2] * j[2][1])
        - j[0][1] * (j[1][0] * j[2][2] - j[1][2] * j[2][0])
        + j[0][2] * (j[1][0] * j[2][1] - j[1][1] * j[2][0])
    )
    r = -det
    inv_ref[0:1, :] = p
    inv_ref[1:2, :] = q
    inv_ref[2:3, :] = r
    inv_ref[3:4, :] = q * q * q + 6.75 * r * r


def shards(sizes, core_tensor, factor_x, factor_y, factor_z, suspect_voxel_list):
    nx, ny, nz = sizes
    comps, ranks_z, ranks_a, ranks_b = core_tensor.shape
    planes = factor_z.shape[0]
    own = planes // nz
    chunk = own // HALVES
    cells_x, cells_y = factor_x.shape[0], factor_y.shape[0]
    ranks_x, ranks_y = factor_x.shape[1], factor_y.shape[1]
    rows = cells_x + SUB
    chunks = comps * HALVES
    count = suspect_voxel_list.shape[1]
    vmem = pl.BlockSpec(memory_space=pltpu.VMEM)
    dma = pltpu.SemaphoreType.DMA
    wide, fy_halo = pl.pallas_call(
        functools.partial(exchange_kernel, sizes),
        out_shape=(
            jax.ShapeDtypeStruct((ny, comps, own + 2, rows, ranks_b), F32),
            jax.ShapeDtypeStruct((2, SUB, ranks_y), F32),
        ),
        in_specs=[pl.BlockSpec(memory_space=pl.ANY), vmem, vmem, vmem],
        out_specs=(vmem, vmem),
        scratch_shapes=[
            pltpu.VMEM((comps, ranks_z, ranks_a, ranks_b), F32),
            pltpu.VMEM((comps, planes, ranks_a, ranks_b), F32),
            pltpu.VMEM((comps, own, ranks_a, ranks_b), F32),
            pltpu.VMEM((chunks, nx, chunk, ranks_a, ranks_b), F32),
            pltpu.VMEM((2, SUB, ranks_x), F32),
            pltpu.VMEM((2 * planes * SUB, ranks_z * SUB), BF16),
            pltpu.VMEM((2 * (cells_x + 2 * SUB), ranks_x), BF16),
            dma((comps,)),
            dma((comps,)),
            dma((comps,)),
            dma((chunks, nx)),
            dma((chunks, nx)),
            dma((chunks, nx)),
            dma((chunks, max(ny - 1, 1))),
            dma((chunks, max(ny - 1, 1))),
            dma((comps, ny)),
            dma((comps, ny)),
            dma((2, 2)),
            dma((2, 2)),
        ],
        compiler_params=pltpu.CompilerParams(
            collective_id=0, has_side_effects=True, vmem_limit_bytes=52 * 2**20
        ),
    )(core_tensor, factor_x, factor_y, factor_z)
    field, invariants = pl.pallas_call(
        functools.partial(field_kernel, cells_x, cells_y),
        out_shape=(
            jax.ShapeDtypeStruct((comps, own, cells_x, cells_y), F32),
            jax.ShapeDtypeStruct((4, count), F32),
        ),
        in_specs=[vmem, vmem, vmem, pl.BlockSpec(memory_space=pltpu.SMEM)],
        out_specs=(vmem, vmem),
        scratch_shapes=[
            pltpu.VMEM(((own + 2) * (cells_x + 2) * SUB, 128), F32),
            pltpu.VMEM(((cells_y + 2) * SUB, 128), F32),
            pltpu.VMEM((3, count * SUB, 128), F32),
        ],
        compiler_params=pltpu.CompilerParams(vmem_limit_bytes=52 * 2**20),
    )(wide, factor_y, fy_halo, suspect_voxel_list)
    return field, invariants


def solution(mesh):
    placed = (
        P("grp", "gz", "gx", "gy"),
        P("gx", "grp"),
        P("gy", "grp"),
        P("grp", "gz"),
        P(("gx", "gy", "gz"), "grp"),
    )
    sizes = (mesh.shape["gx"], mesh.shape["gy"], mesh.shape["gz"])
    return jax.shard_map(
        functools.partial(shards, sizes),
        mesh=mesh,
        in_specs=placed,
        out_specs=(P("grp", "gz", "gx", "gy"), P("grp", ("gx", "gy", "gz"))),
        check_vma=False,
    )
```

```python
import functools

import jax
import jax.numpy as jnp
from jax import lax
from jax.experimental import pallas as pl
from jax.experimental.pallas import tpu as pltpu
from jax.sharding import PartitionSpec as P

MESH = pl.DeviceIdType.MESH
F32 = jnp.float32
BF16 = jnp.bfloat16
SUB = 8
HALVES = 4
AHEAD = 3


def split(value):
    high = value.astype(BF16)
    return high, (value - high.astype(F32)).astype(BF16)


def dot(left, right):
    return jnp.dot(left, right, preferred_element_type=F32)


def dot_last(left, right):
    return lax.dot_general(left, right, (((1,), (1,)), ((), ())), preferred_element_type=F32)


def exchange_kernel(
    sizes, core_hbm, fx_hbm, fy_ref, fz_hbm, wide_ref, fy_halo_ref,
    fx_ref, fz_ref, fx_end_ref, fx_end_ref2, partial_ref, load_sem, end_send, end_recv,
    partial_send, partial_recv, core_ref, part_ref, pair_ref, slab_ref, fx_halo_ref, kron_ref, fx_ref2,
    core_sem, pair_send, pair_recv, right_send, left_send, slab_recv,
    y_send, y_recv, z_send, z_recv, edge_send, edge_recv,
):
    nx, ny, nz = sizes
    comps, ranks_z, ranks_a, ranks_b = core_ref.shape
    planes = part_ref.shape[1]
    own = planes // nz
    chunk = own // HALVES
    cells_x = fx_ref.shape[0]
    rows = wide_ref.shape[3]
    px = lax.axis_index("gx")
    py = lax.axis_index("gy")
    pz = lax.axis_index("gz")

    loads = [
        pltpu.make_async_copy(source, target, load_sem.at[index])
        for index, (source, target) in enumerate(((fz_hbm, fz_ref), (fx_hbm, fx_ref)))
    ]
    for load in loads:
        load.start()
    for c in range(comps):
        pltpu.make_async_copy(core_hbm.at[c], core_ref.at[c], core_sem.at[c]).start()

    fx_halo_ref[...] = jnp.zeros_like(fx_halo_ref)
    fy_halo_ref[...] = jnp.zeros_like(fy_halo_ref)
    wide_ref[:, :, pl.ds(own + 1 - pz, 1)] = jnp.zeros(
        (ny, comps, 1, rows, ranks_b), F32
    )

    has_left, has_right = px > 0, px < nx - 1
    ends = nx >= 4 and (nx - 1) * ranks_a > rows
    if ends:
        feeds_left, feeds_right = px > 1, px < nx - 2
        is_first, is_last = px == 0, px == nx - 1
    else:
        feeds_left, feeds_right = has_left, has_right
    below, above = py > 0, py < ny - 1
    partner = {"gz": 1 - pz}
    barrier = pltpu.get_barrier_semaphore()

    @pl.when(has_left)
    def _():
        pl.semaphore_signal(barrier, inc=1, device_id={"gx": px - 1}, device_id_type=MESH)

    @pl.when(has_right)
    def _():
        pl.semaphore_signal(barrier, inc=1, device_id={"gx": px + 1}, device_id_type=MESH)

    for step in range(1, ny):
        pl.semaphore_signal(
            barrier, inc=1, device_id={"gy": lax.rem(py + step, ny)}, device_id_type=MESH
        )
    pl.semaphore_signal(barrier, inc=1, device_id=partner, device_id_type=MESH)

    loads[0].wait()
    zh, zl = split(fz_ref[...])
    tall = planes * SUB
    wide = ranks_z * SUB
    spread = (
        lax.broadcasted_iota(jnp.int32, (tall, planes), 0) // SUB
        == lax.broadcasted_iota(jnp.int32, (tall, planes), 1)
    ).astype(F32).astype(BF16)
    repeat = (
        lax.broadcasted_iota(jnp.int32, (ranks_z, wide), 1) // SUB
        == lax.broadcasted_iota(jnp.int32, (ranks_z, wide), 0)
    ).astype(F32).astype(BF16)
    same = (
        lax.broadcasted_iota(jnp.int32, (tall, wide), 0) % SUB
        == lax.broadcasted_iota(jnp.int32, (tall, wide), 1) % SUB
    )
    for index, piece in enumerate((zh, zl)):
        grown = dot(dot(spread, piece).astype(BF16), repeat)
        kron_ref[index * tall : (index + 1) * tall] = jnp.where(same, grown, 0.0).astype(BF16)

    greeted = has_left.astype(jnp.int32) + has_right.astype(jnp.int32) + ny
    pl.semaphore_wait(barrier, greeted)

    edges = []
    for index, (axis, at, low, high, source, target) in enumerate((
        ("gx", px, has_left, has_right, fx_hbm, fx_halo_ref),
        ("gy", py, below, above, fy_ref, fy_halo_ref),
    )):
        last = source.shape[0] - SUB
        up = pltpu.make_async_remote_copy(
            source.at[pl.ds(last, SUB)], target.at[0], edge_send.at[index, 0],
            edge_recv.at[index, 0], device_id={axis: at + 1}, device_id_type=MESH,
        )
        down = pltpu.make_async_remote_copy(
            source.at[pl.ds(0, SUB)], target.at[1], edge_send.at[index, 1],
            edge_recv.at[index, 1], device_id={axis: at - 1}, device_id_type=MESH,
        )
        pl.when(high)(up.start)
        pl.when(low)(down.start)
        edges.append((low, high, up, down))

    def end_copy(target):
        return pltpu.make_async_remote_copy(
            fx_hbm, fx_end_ref, end_send, end_recv, device_id={"gx": target},
            device_id_type=MESH,
        )

    if ends:
        pl.when(is_first)(end_copy(1).start)
        pl.when(is_last)(end_copy(nx - 2).start)

    def pair_copy(c):
        return pltpu.make_async_remote_copy(
            part_ref.at[c, pl.ds((1 - pz) * own, own)], pair_ref.at[c], pair_send.at[c],
            pair_recv.at[c], device_id=partner, device_id_type=MESH,
        )

    def slab_copy(q, origin, sem, target):
        return pltpu.make_async_remote_copy(
            slab_ref.at[q, origin], slab_ref.at[q, origin], sem.at[q, origin],
            slab_recv.at[q, origin], device_id={"gx": target}, device_id_type=MESH,
        )

    def contract_z(c):
        pltpu.make_async_copy(core_hbm.at[c], core_ref.at[c], core_sem.at[c]).wait()

        def body(step, carry):
            first = pl.multiple_of(step * 2 * SUB, SUB)
            both = jnp.concatenate(
                [
                    core_ref[c, :, pl.ds(first + at, SUB), :].reshape(wide, ranks_b)
                    for at in (0, SUB)
                ],
                axis=1,
            )
            high, low = split(both)
            stacked = dot(kron_ref[...], high)
            out = stacked[:tall] + stacked[tall:] + dot(kron_ref[:tall], low)
            for index, at in enumerate((0, SUB)):
                part_ref[c, :, pl.ds(first + at, SUB), :] = out[
                    :, index * ranks_b : (index + 1) * ranks_b
                ].reshape(planes, SUB, ranks_b)
            return carry

        lax.fori_loop(0, ranks_a // (2 * SUB), body, 0)
        pair_copy(c).start()

    def finish_z(c):
        pair_copy(c).wait_recv()
        for half in range(HALVES):
            q = c * HALVES + half
            slab_ref[q, px] = (
                part_ref[c, pl.ds(pz * own + half * chunk, chunk)]
                + pair_ref[c, half * chunk : (half + 1) * chunk]
            )

    def send_own(q):
        @pl.when(feeds_right)
        def _():
            slab_copy(q, px, right_send, px + 1).start()

        @pl.when(feeds_left)
        def _():
            slab_copy(q, px, left_send, px - 1).start()

    contract_z(0)
    for c in range(1, comps):
        contract_z(c)
        finish_z(c - 1)
        if c == 1:
            for q in range(AHEAD):
                send_own(q)
    finish_z(comps - 1)
    loads[1].wait()

    for low, high, up, down in edges:
        pl.when(low)(up.wait_recv)
        pl.when(high)(down.wait_recv)
    tile = lax.broadcasted_iota(jnp.int32, (2 * SUB, fx_ref.shape[1]), 0)
    outer = jnp.where(
        tile == 0, fx_halo_ref[0, SUB - 1 : SUB, :],
        jnp.where(tile == 1, fx_halo_ref[1, 0:1, :], 0.0),
    )
    full = cells_x + 2 * SUB
    xh, xl = split(jnp.concatenate([fx_ref[...], outer], axis=0))
    fx_ref2[:full] = xh
    fx_ref2[full:] = xl

    def prepare_end(row, index):
        end_copy(px).wait_recv()
        extra = jnp.where(tile == index, row, 0.0)
        eh, el = split(jnp.concatenate([fx_end_ref[...], extra], axis=0))
        fx_end_ref2[:full] = eh
        fx_end_ref2[full:] = el

    if ends:
        @pl.when(px == 1)
        def _():
            prepare_end(fx_ref[0:1, :], 1)

        @pl.when(px == nx - 2)
        def _():
            prepare_end(fx_ref[cells_x - 1 : cells_x, :], 0)

    def y_copy(q, step):
        c, half = q // HALVES, q % HALVES
        block = wide_ref.at[py, c, pl.ds(half * chunk, chunk)]
        return pltpu.make_async_remote_copy(
            block, block, y_send.at[q, step - 1], y_recv.at[q, step - 1],
            device_id={"gy": lax.rem(py + step, ny)}, device_id_type=MESH,
        )

    def y_arrived(q, step):
        c, half = q // HALVES, q % HALVES
        block = wide_ref.at[lax.rem(py + ny - step, ny), c, pl.ds(half * chunk, chunk)]
        return pltpu.make_async_remote_copy(
            block, block, y_send.at[q, step - 1], y_recv.at[q, step - 1],
            device_id={"gy": lax.rem(py + step, ny)}, device_id_type=MESH,
        )

    def z_copy(c, step):
        owner = lax.rem(py + ny - step, ny)
        edge = (1 - pz) * (own - 1)
        return pltpu.make_async_remote_copy(
            wide_ref.at[owner, c, edge], wide_ref.at[owner, c, own + 1 - pz],
            z_send.at[c, step], z_recv.at[c, step], device_id=partner, device_id_type=MESH,
        )

    def expand(q, factor_ref, keep, emit):
        empty = jnp.zeros((ranks_a, ranks_b), F32)
        for k in range(0, chunk, 2):
            both = jnp.concatenate(
                [
                    jnp.concatenate(
                        [slab_ref[q, o, k + at] if o in keep else empty for o in range(nx)], axis=0
                    )
                    for at in (0, 1)
                ],
                axis=1,
            )
            high, low = split(both)
            stacked = dot(factor_ref[...], high)
            out = stacked[:full] + stacked[full:] + dot(factor_ref[:full], low)
            for at in (0, 1):
                emit(k + at, out[:rows, at * ranks_b : (at + 1) * ranks_b])

    def partial_copy(q, target):
        c, half = q // HALVES, q % HALVES
        return pltpu.make_async_remote_copy(
            partial_ref.at[q], wide_ref.at[py, c, pl.ds(half * chunk, chunk)],
            partial_send.at[q], partial_recv.at[q], device_id={"gx": target},
            device_id_type=MESH,
        )

    everyone = range(nx)
    for q in range(comps * HALVES):
        c, half = q // HALVES, q % HALVES

        def emit_own(k, value):
            wide_ref[py, c, half * chunk + k] = value

        def emit_more(k, value):
            wide_ref[py, c, half * chunk + k] += value

        def emit_partial(k, value):
            partial_ref[q, k] = value

        for hop in range(1, nx):
            @pl.when((px >= hop) & ((px < nx - 1) if ends else True))
            def _():
                slab_copy(q, px - hop, right_send, px).wait_recv()

                @pl.when(feeds_right)
                def _():
                    slab_copy(q, px - hop, right_send, px + 1).start()

            @pl.when((px + hop < nx) & ((px > 0) if ends else True))
            def _():
                slab_copy(q, px + hop, left_send, px).wait_recv()

                @pl.when(feeds_left)
                def _():
                    slab_copy(q, px + hop, left_send, px - 1).start()

        if q + AHEAD < comps * HALVES:
            send_own(q + AHEAD)
        if ends:
            for end, near in ((0, 1), (nx - 1, nx - 2)):
                @pl.when(px == near)
                def _():
                    expand(q, fx_end_ref2, [o for o in everyone if o != end], emit_partial)
                    partial_copy(q, end).start()

            @pl.when(has_left & has_right)
            def _():
                expand(q, fx_ref2, everyone, emit_own)

            for end in (0, nx - 1):
                @pl.when(px == end)
                def _():
                    partial_copy(q, end).wait_recv()
                    expand(q, fx_ref2, [end], emit_more)
        else:
            expand(q, fx_ref2, everyone, emit_own)
        for step in range(1, ny):
            y_copy(q, step).start()
        if half == HALVES - 1:
            z_copy(c, 0).start()

    for c in range(comps):
        for step in range(1, ny):
            for half in range(HALVES):
                y_arrived(c * HALVES + half, step).wait_recv()
            z_copy(c, step).start()

    if ends:
        pl.when(is_first)(end_copy(1).wait_send)
        pl.when(is_last)(end_copy(nx - 2).wait_send)
    for low, high, up, down in edges:
        pl.when(high)(up.wait_send)
        pl.when(low)(down.wait_send)
    for c in range(comps):
        pair_copy(c).wait_send()
    for q in range(comps * HALVES):
        for origin in range(nx):
            @pl.when((origin <= px) & feeds_right)
            def _():
                slab_copy(q, origin, right_send, px + 1).wait_send()

            @pl.when((origin >= px) & feeds_left)
            def _():
                slab_copy(q, origin, left_send, px - 1).wait_send()
        for step in range(1, ny):
            y_copy(q, step).wait_send()
        if ends:
            for end, near in ((0, 1), (nx - 1, nx - 2)):
                @pl.when(px == near)
                def _():
                    partial_copy(q, end).wait_send()
    for c in range(comps):
        for step in range(ny):
            z_copy(c, step).wait_send()
            z_copy(c, step).wait_recv()


def field_kernel(
    cells_x, cells_y, wide_ref, fy_ref, fy_halo_ref, list_ref, field_ref, inv_ref,
    rows_ref, fy_rows_ref, prod_ref,
):
    ny, comps, slots, _, ranks_b = wide_ref.shape
    own = slots - 2
    ranks = ny * ranks_b
    lanes = 128
    parts = ranks // lanes
    count = list_ref.shape[1]
    per_plane = cells_x + 2

    def joined(c, k, start, size):
        return jnp.concatenate(
            [wide_ref[y, c, k, start : start + size, :] for y in range(ny)], axis=1
        )

    for c in range(comps):
        for k in range(slots):
            spot = 0 if k == own + 1 else k + 1
            base = spot * per_plane * SUB
            inner = joined(c, k, 0, cells_x)
            outer = joined(c, k, cells_x, SUB)
            for part in range(parts):
                cut = slice(part * lanes, (part + 1) * lanes)
                lane = c * parts + part
                rows_ref[pl.ds(base + SUB + lane, cells_x, stride=SUB), :] = inner[:, cut]
                rows_ref[pl.ds(base + lane, 1), :] = outer[0:1, cut]
                rows_ref[pl.ds(base + (cells_x + 1) * SUB + lane, 1), :] = outer[1:2, cut]
    for c in range(comps):
        for part in range(parts):
            cut = slice(part * lanes, (part + 1) * lanes)
            lane = c * parts + part
            fy_rows_ref[pl.ds(SUB + lane, cells_y, stride=SUB), :] = fy_ref[:, cut]
            fy_rows_ref[pl.ds(lane, 1), :] = fy_halo_ref[0, SUB - 1 : SUB, cut]
            fy_rows_ref[pl.ds((cells_y + 1) * SUB + lane, 1), :] = fy_halo_ref[1, 0:1, cut]

    def candidate(n, carry):
        cell = list_ref[0, n]
        plane = cell // (cells_x * cells_y)
        row = cell // cells_y % cells_x
        column = cell % cells_y
        spot = (plane + 1) * per_plane + row + 1

        def at(ref, index):
            return ref[pl.ds(pl.multiple_of(index * SUB, SUB), SUB), :]

        centre = at(fy_rows_ref, column + 1)
        here = pl.ds(pl.multiple_of(n * SUB, SUB), SUB)
        prod_ref[0, here, :] = (at(rows_ref, spot + 1) - at(rows_ref, spot - 1)) * centre
        prod_ref[1, here, :] = at(rows_ref, spot) * (
            at(fy_rows_ref, column + 2) - at(fy_rows_ref, column)
        )
        prod_ref[2, here, :] = (
            at(rows_ref, spot + per_plane) - at(rows_ref, spot - per_plane)
        ) * centre
        return carry

    lax.fori_loop(0, count, candidate, 0, unroll=8)

    fh, fl = split(fy_ref[...])
    for c in range(comps):
        flat = jnp.concatenate(
            [
                wide_ref[y, c, 0:own, 0:cells_x, :].reshape(own * cells_x, ranks_b)
                for y in range(ny)
            ],
            axis=1,
        )
        high, low = split(flat)
        out = dot_last(high, fh) + dot_last(high, fl) + dot_last(low, fh)
        field_ref[c] = out.reshape(own, cells_x, cells_y)

    ones = jnp.ones((SUB * 2, lanes), F32).astype(BF16)

    def grad(c, d):
        total = prod_ref[d, pl.ds(c * parts, count, stride=SUB), :]
        for part in range(1, parts):
            total = total + prod_ref[d, pl.ds(c * parts + part, count, stride=SUB), :]
        high, low = split(total)
        return 0.5 * (dot_last(ones, high) + dot_last(ones, low))[0:1, :]

    j = [[grad(c, d) for d in range(3)] for c in range(3)]
    p = -(j[0][0] + j[1][1] + j[2][2])
    square = j[0][0] * j[0][0]
    for a in range(3):
        for b in range(3):
            if a + b > 0:
                square = square + j[a][b] * j[b][a]
    q = 0.5 * (p * p - square)
    det = (
        j[0][0] * (j[1][1] * j[2][2] - j[1][2] * j[2][1])
        - j[0][1] * (j[1][0] * j[2][2] - j[1][2] * j[2][0])
        + j[0][2] * (j[1][0] * j[2][1] - j[1][1] * j[2][0])
    )
    r = -det
    inv_ref[0:1, :] = p
    inv_ref[1:2, :] = q
    inv_ref[2:3, :] = r
    inv_ref[3:4, :] = q * q * q + 6.75 * r * r


def shards(sizes, core_tensor, factor_x, factor_y, factor_z, suspect_voxel_list):
    nx, ny, nz = sizes
    comps, ranks_z, ranks_a, ranks_b = core_tensor.shape
    planes = factor_z.shape[0]
    own = planes // nz
    chunk = own // HALVES
    cells_x, cells_y = factor_x.shape[0], factor_y.shape[0]
    ranks_x, ranks_y = factor_x.shape[1], factor_y.shape[1]
    rows = cells_x + SUB
    chunks = comps * HALVES
    count = suspect_voxel_list.shape[1]
    vmem = pl.BlockSpec(memory_space=pltpu.VMEM)
    dma = pltpu.SemaphoreType.DMA
    wide, fy_halo = pl.pallas_call(
        functools.partial(exchange_kernel, sizes),
        out_shape=(
            jax.ShapeDtypeStruct((ny, comps, own + 2, rows, ranks_b), F32),
            jax.ShapeDtypeStruct((2, SUB, ranks_y), F32),
        ),
        in_specs=[pl.BlockSpec(memory_space=pl.ANY)] * 4,
        out_specs=(vmem, vmem),
        scratch_shapes=[
            pltpu.VMEM((cells_x, ranks_x), F32),
            pltpu.VMEM((planes, ranks_z), F32),
            pltpu.VMEM((cells_x, ranks_x), F32),
            pltpu.VMEM((2 * (cells_x + 2 * SUB), ranks_x), BF16),
            pltpu.VMEM((chunks, chunk, rows, ranks_b), F32),
            dma((2,)),
            dma,
            dma,
            dma((chunks,)),
            dma((chunks,)),
            pltpu.VMEM((comps, ranks_z, ranks_a, ranks_b), F32),
            pltpu.VMEM((comps, planes, ranks_a, ranks_b), F32),
            pltpu.VMEM((comps, own, ranks_a, ranks_b), F32),
            pltpu.VMEM((chunks, nx, chunk, ranks_a, ranks_b), F32),
            pltpu.VMEM((2, SUB, ranks_x), F32),
            pltpu.VMEM((2 * planes * SUB, ranks_z * SUB), BF16),
            pltpu.VMEM((2 * (cells_x + 2 * SUB), ranks_x), BF16),
            dma((comps,)),
            dma((comps,)),
            dma((comps,)),
            dma((chunks, nx)),
            dma((chunks, nx)),
            dma((chunks, nx)),
            dma((chunks, max(ny - 1, 1))),
            dma((chunks, max(ny - 1, 1))),
            dma((comps, ny)),
            dma((comps, ny)),
            dma((2, 2)),
            dma((2, 2)),
        ],
        compiler_params=pltpu.CompilerParams(
            collective_id=0, has_side_effects=True, vmem_limit_bytes=52 * 2**20
        ),
    )(core_tensor, factor_x, factor_y, factor_z)
    field, invariants = pl.pallas_call(
        functools.partial(field_kernel, cells_x, cells_y),
        out_shape=(
            jax.ShapeDtypeStruct((comps, own, cells_x, cells_y), F32),
            jax.ShapeDtypeStruct((4, count), F32),
        ),
        in_specs=[vmem, vmem, vmem, pl.BlockSpec(memory_space=pltpu.SMEM)],
        out_specs=(vmem, vmem),
        scratch_shapes=[
            pltpu.VMEM(((own + 2) * (cells_x + 2) * SUB, 128), F32),
            pltpu.VMEM(((cells_y + 2) * SUB, 128), F32),
            pltpu.VMEM((3, count * SUB, 128), F32),
        ],
        compiler_params=pltpu.CompilerParams(vmem_limit_bytes=52 * 2**20),
    )(wide, factor_y, fy_halo, suspect_voxel_list)
    return field, invariants


def solution(mesh):
    placed = (
        P("grp", "gz", "gx", "gy"),
        P("gx", "grp"),
        P("gy", "grp"),
        P("grp", "gz"),
        P(("gx", "gy", "gz"), "grp"),
    )
    sizes = (mesh.shape["gx"], mesh.shape["gy"], mesh.shape["gz"])
    return jax.shard_map(
        functools.partial(shards, sizes),
        mesh=mesh,
        in_specs=placed,
        out_specs=(P("grp", "gz", "gx", "gy"), P("grp", ("gx", "gy", "gz"))),
        check_vma=False,
    )
```

```python
import functools

import jax
import jax.numpy as jnp
from jax import lax
from jax.experimental import pallas as pl
from jax.experimental.pallas import tpu as pltpu
from jax.sharding import PartitionSpec as P

MESH = pl.DeviceIdType.MESH
F32 = jnp.float32
BF16 = jnp.bfloat16
SUB = 8
HALVES = 4
AHEAD = 4
SKEW = 2


def split(value):
    high = value.astype(BF16)
    return high, (value - high.astype(F32)).astype(BF16)


def dot(left, right):
    return jnp.dot(left, right, preferred_element_type=F32)


def dot_last(left, right):
    return lax.dot_general(left, right, (((1,), (1,)), ((), ())), preferred_element_type=F32)


def exchange_kernel(
    sizes, core_hbm, fx_hbm, fy_ref, fz_hbm, wide_ref, fy_halo_ref,
    fx_ref, fz_ref, fx_end_ref, fx_end_ref2, partial_ref, load_sem, end_send, end_recv,
    partial_send, partial_recv, core_ref, part_ref, pair_ref, slab_ref, fx_halo_ref, kron_ref, fx_ref2,
    core_sem, pair_send, pair_recv, right_send, left_send, slab_recv,
    y_send, y_recv, z_send, z_recv, edge_send, edge_recv,
):
    nx, ny, nz = sizes
    comps, ranks_z, ranks_a, ranks_b = core_ref.shape
    planes = part_ref.shape[1]
    own = planes // nz
    chunk = own // HALVES
    cells_x = fx_ref.shape[0]
    rows = wide_ref.shape[3]
    px = lax.axis_index("gx")
    py = lax.axis_index("gy")
    pz = lax.axis_index("gz")

    loads = [
        pltpu.make_async_copy(source, target, load_sem.at[index])
        for index, (source, target) in enumerate(((fz_hbm, fz_ref), (fx_hbm, fx_ref)))
    ]
    for load in loads:
        load.start()
    for c in range(comps):
        pltpu.make_async_copy(core_hbm.at[c], core_ref.at[c], core_sem.at[c]).start()

    fx_halo_ref[...] = jnp.zeros_like(fx_halo_ref)
    fy_halo_ref[...] = jnp.zeros_like(fy_halo_ref)
    wide_ref[:, :, pl.ds(own + 1 - pz, 1)] = jnp.zeros(
        (ny, comps, 1, rows, ranks_b), F32
    )

    has_left, has_right = px > 0, px < nx - 1
    ends = nx >= 4 and (nx - 1) * ranks_a > rows
    if ends:
        feeds_left, feeds_right = px > 1, px < nx - 2
        is_first, is_last = px == 0, px == nx - 1
    else:
        feeds_left, feeds_right = has_left, has_right
    below, above = py > 0, py < ny - 1
    partner = {"gz": 1 - pz}
    barrier = pltpu.get_barrier_semaphore()

    @pl.when(has_left)
    def _():
        pl.semaphore_signal(barrier, inc=1, device_id={"gx": px - 1}, device_id_type=MESH)

    @pl.when(has_right)
    def _():
        pl.semaphore_signal(barrier, inc=1, device_id={"gx": px + 1}, device_id_type=MESH)

    for step in range(1, ny):
        pl.semaphore_signal(
            barrier, inc=1, device_id={"gy": lax.rem(py + step, ny)}, device_id_type=MESH
        )
    pl.semaphore_signal(barrier, inc=1, device_id=partner, device_id_type=MESH)

    loads[0].wait()
    zh, zl = split(fz_ref[...])
    tall = planes * SUB
    wide = ranks_z * SUB
    spread = (
        lax.broadcasted_iota(jnp.int32, (tall, planes), 0) // SUB
        == lax.broadcasted_iota(jnp.int32, (tall, planes), 1)
    ).astype(F32).astype(BF16)
    repeat = (
        lax.broadcasted_iota(jnp.int32, (ranks_z, wide), 1) // SUB
        == lax.broadcasted_iota(jnp.int32, (ranks_z, wide), 0)
    ).astype(F32).astype(BF16)
    same = (
        lax.broadcasted_iota(jnp.int32, (tall, wide), 0) % SUB
        == lax.broadcasted_iota(jnp.int32, (tall, wide), 1) % SUB
    )
    for index, piece in enumerate((zh, zl)):
        grown = dot(dot(spread, piece).astype(BF16), repeat)
        kron_ref[index * tall : (index + 1) * tall] = jnp.where(same, grown, 0.0).astype(BF16)

    greeted = has_left.astype(jnp.int32) + has_right.astype(jnp.int32) + ny
    pl.semaphore_wait(barrier, greeted)

    edges = []
    for index, (axis, at, low, high, source, target) in enumerate((
        ("gx", px, has_left, has_right, fx_hbm, fx_halo_ref),
        ("gy", py, below, above, fy_ref, fy_halo_ref),
    )):
        last = source.shape[0] - SUB
        up = pltpu.make_async_remote_copy(
            source.at[pl.ds(last, SUB)], target.at[0], edge_send.at[index, 0],
            edge_recv.at[index, 0], device_id={axis: at + 1}, device_id_type=MESH,
        )
        down = pltpu.make_async_remote_copy(
            source.at[pl.ds(0, SUB)], target.at[1], edge_send.at[index, 1],
            edge_recv.at[index, 1], device_id={axis: at - 1}, device_id_type=MESH,
        )
        pl.when(high)(up.start)
        pl.when(low)(down.start)
        edges.append((low, high, up, down))

    def end_copy(target):
        return pltpu.make_async_remote_copy(
            fx_hbm, fx_end_ref, end_send, end_recv, device_id={"gx": target},
            device_id_type=MESH,
        )

    if ends:
        pl.when(is_first)(end_copy(1).start)
        pl.when(is_last)(end_copy(nx - 2).start)

    def pair_copy(c):
        return pltpu.make_async_remote_copy(
            part_ref.at[c, pl.ds((1 - pz) * own, own)], pair_ref.at[c], pair_send.at[c],
            pair_recv.at[c], device_id=partner, device_id_type=MESH,
        )

    def slab_copy(q, origin, sem, target):
        return pltpu.make_async_remote_copy(
            slab_ref.at[q, origin], slab_ref.at[q, origin], sem.at[q, origin],
            slab_recv.at[q, origin], device_id={"gx": target}, device_id_type=MESH,
        )

    def contract_z(c):
        pltpu.make_async_copy(core_hbm.at[c], core_ref.at[c], core_sem.at[c]).wait()

        def body(step, carry):
            first = pl.multiple_of(step * 2 * SUB, SUB)
            both = jnp.concatenate(
                [
                    core_ref[c, :, pl.ds(first + at, SUB), :].reshape(wide, ranks_b)
                    for at in (0, SUB)
                ],
                axis=1,
            )
            high, low = split(both)
            stacked = dot(kron_ref[...], high)
            out = stacked[:tall] + stacked[tall:] + dot(kron_ref[:tall], low)
            for index, at in enumerate((0, SUB)):
                part_ref[c, :, pl.ds(first + at, SUB), :] = out[
                    :, index * ranks_b : (index + 1) * ranks_b
                ].reshape(planes, SUB, ranks_b)
            return carry

        lax.fori_loop(0, ranks_a // (2 * SUB), body, 0)
        pair_copy(c).start()

    def send_own(q):
        @pl.when(feeds_right)
        def _():
            slab_copy(q, px, right_send, px + 1).start()

        @pl.when(feeds_left)
        def _():
            slab_copy(q, px, left_send, px - 1).start()

    def send_next(q):
        if ends:
            pl.when(has_left & has_right)(functools.partial(send_own, q))
        else:
            send_own(q)

    def finish_z(c):
        pair_copy(c).wait_recv()
        for half in range(HALVES):
            q = c * HALVES + half
            slab_ref[q, px] = (
                part_ref[c, pl.ds(pz * own + half * chunk, chunk)]
                + pair_ref[c, half * chunk : (half + 1) * chunk]
            )
            if ends:
                pl.when(is_first | is_last)(functools.partial(send_own, q))

    contract_z(0)
    for c in range(1, comps):
        contract_z(c)
        finish_z(c - 1)
        if c == 1:
            for q in range(AHEAD):
                send_next(q)
    finish_z(comps - 1)
    loads[1].wait()

    for low, high, up, down in edges:
        pl.when(low)(up.wait_recv)
        pl.when(high)(down.wait_recv)
    tile = lax.broadcasted_iota(jnp.int32, (2 * SUB, fx_ref.shape[1]), 0)
    outer = jnp.where(
        tile == 0, fx_halo_ref[0, SUB - 1 : SUB, :],
        jnp.where(tile == 1, fx_halo_ref[1, 0:1, :], 0.0),
    )
    full = cells_x + 2 * SUB
    xh, xl = split(jnp.concatenate([fx_ref[...], outer], axis=0))
    fx_ref2[:full] = xh
    fx_ref2[full:] = xl

    def prepare_end(row, index):
        end_copy(px).wait_recv()
        extra = jnp.where(tile == index, row, 0.0)
        eh, el = split(jnp.concatenate([fx_end_ref[...], extra], axis=0))
        fx_end_ref2[:full] = eh
        fx_end_ref2[full:] = el

    if ends:
        @pl.when(px == 1)
        def _():
            prepare_end(fx_ref[0:1, :], 1)

        @pl.when(px == nx - 2)
        def _():
            prepare_end(fx_ref[cells_x - 1 : cells_x, :], 0)

    def y_copy(q, step):
        c, half = q // HALVES, q % HALVES
        block = wide_ref.at[py, c, pl.ds(half * chunk, chunk)]
        return pltpu.make_async_remote_copy(
            block, block, y_send.at[q, step - 1], y_recv.at[q, step - 1],
            device_id={"gy": lax.rem(py + step, ny)}, device_id_type=MESH,
        )

    def y_arrived(q, step):
        c, half = q // HALVES, q % HALVES
        block = wide_ref.at[lax.rem(py + ny - step, ny), c, pl.ds(half * chunk, chunk)]
        return pltpu.make_async_remote_copy(
            block, block, y_send.at[q, step - 1], y_recv.at[q, step - 1],
            device_id={"gy": lax.rem(py + step, ny)}, device_id_type=MESH,
        )

    def z_copy(c, step):
        owner = lax.rem(py + ny - step, ny)
        edge = (1 - pz) * (own - 1)
        return pltpu.make_async_remote_copy(
            wide_ref.at[owner, c, edge], wide_ref.at[owner, c, own + 1 - pz],
            z_send.at[c, step], z_recv.at[c, step], device_id=partner, device_id_type=MESH,
        )

    def expand(q, factor_ref, keep, emit):
        empty = jnp.zeros((ranks_a, ranks_b), F32)
        for k in range(0, chunk, 2):
            both = jnp.concatenate(
                [
                    jnp.concatenate(
                        [slab_ref[q, o, k + at] if o in keep else empty for o in range(nx)], axis=0
                    )
                    for at in (0, 1)
                ],
                axis=1,
            )
            high, low = split(both)
            stacked = dot(factor_ref[...], high)
            out = stacked[:full] + stacked[full:] + dot(factor_ref[:full], low)
            for at in (0, 1):
                emit(k + at, out[:rows, at * ranks_b : (at + 1) * ranks_b])

    def partial_copy(q, target):
        c, half = q // HALVES, q % HALVES
        return pltpu.make_async_remote_copy(
            partial_ref.at[q], wide_ref.at[py, c, pl.ds(half * chunk, chunk)],
            partial_send.at[q], partial_recv.at[q], device_id={"gx": target},
            device_id_type=MESH,
        )

    everyone = range(nx)
    total = comps * HALVES
    hops = nx - 2 if ends else nx - 1

    def relay(q, hop):
        @pl.when((px >= hop) & ((px < nx - 1) if ends else True))
        def _():
            slab_copy(q, px - hop, right_send, px).wait_recv()

            @pl.when(feeds_right)
            def _():
                slab_copy(q, px - hop, right_send, px + 1).start()

        @pl.when((px + hop < nx) & ((px > 0) if ends else True))
        def _():
            slab_copy(q, px + hop, left_send, px).wait_recv()

            @pl.when(feeds_left)
            def _():
                slab_copy(q, px + hop, left_send, px - 1).start()

    def consume(q):
        c, half = q // HALVES, q % HALVES

        def emit_own(k, value):
            wide_ref[py, c, half * chunk + k] = value

        def emit_more(k, value):
            wide_ref[py, c, half * chunk + k] += value

        def emit_partial(k, value):
            partial_ref[q, k] = value

        if ends:
            for end, near in ((0, 1), (nx - 1, nx - 2)):
                @pl.when(px == near)
                def _():
                    expand(q, fx_end_ref2, [o for o in everyone if o != end], emit_partial)
                    partial_copy(q, end).start()

            @pl.when(has_left & has_right)
            def _():
                expand(q, fx_ref2, everyone, emit_own)

            for end in (0, nx - 1):
                @pl.when(px == end)
                def _():
                    partial_copy(q, end).wait_recv()
                    expand(q, fx_ref2, [end], emit_more)
        else:
            expand(q, fx_ref2, everyone, emit_own)
        for step in range(1, ny):
            y_copy(q, step).start()
        if half == HALVES - 1:
            z_copy(c, 0).start()

    for turn in range(total + SKEW * (hops - 1)):
        for hop in range(1, hops + 1):
            q = turn - SKEW * (hop - 1)
            if 0 <= q < total:
                relay(q, hop)
        if turn + AHEAD < total:
            send_next(turn + AHEAD)
        if turn >= SKEW * (hops - 1):
            consume(turn - SKEW * (hops - 1))

    for c in range(comps):
        for step in range(1, ny):
            for half in range(HALVES):
                y_arrived(c * HALVES + half, step).wait_recv()
            z_copy(c, step).start()

    if ends:
        pl.when(is_first)(end_copy(1).wait_send)
        pl.when(is_last)(end_copy(nx - 2).wait_send)
    for low, high, up, down in edges:
        pl.when(high)(up.wait_send)
        pl.when(low)(down.wait_send)
    for c in range(comps):
        pair_copy(c).wait_send()
    for q in range(comps * HALVES):
        for origin in range(nx):
            @pl.when((origin <= px) & feeds_right)
            def _():
                slab_copy(q, origin, right_send, px + 1).wait_send()

            @pl.when((origin >= px) & feeds_left)
            def _():
                slab_copy(q, origin, left_send, px - 1).wait_send()
        for step in range(1, ny):
            y_copy(q, step).wait_send()
        if ends:
            for end, near in ((0, 1), (nx - 1, nx - 2)):
                @pl.when(px == near)
                def _():
                    partial_copy(q, end).wait_send()
    for c in range(comps):
        for step in range(ny):
            z_copy(c, step).wait_send()
            z_copy(c, step).wait_recv()


def field_kernel(
    cells_x, cells_y, wide_ref, fy_ref, fy_halo_ref, list_ref, field_ref, inv_ref,
    rows_ref, fy_rows_ref, prod_ref,
):
    ny, comps, slots, _, ranks_b = wide_ref.shape
    own = slots - 2
    ranks = ny * ranks_b
    lanes = 128
    parts = ranks // lanes
    count = list_ref.shape[1]
    per_plane = cells_x + 2

    def joined(c, k, start, size):
        return jnp.concatenate(
            [wide_ref[y, c, k, start : start + size, :] for y in range(ny)], axis=1
        )

    for c in range(comps):
        for k in range(slots):
            spot = 0 if k == own + 1 else k + 1
            base = spot * per_plane * SUB
            inner = joined(c, k, 0, cells_x)
            outer = joined(c, k, cells_x, SUB)
            for part in range(parts):
                cut = slice(part * lanes, (part + 1) * lanes)
                lane = c * parts + part
                rows_ref[pl.ds(base + SUB + lane, cells_x, stride=SUB), :] = inner[:, cut]
                rows_ref[pl.ds(base + lane, 1), :] = outer[0:1, cut]
                rows_ref[pl.ds(base + (cells_x + 1) * SUB + lane, 1), :] = outer[1:2, cut]
    for c in range(comps):
        for part in range(parts):
            cut = slice(part * lanes, (part + 1) * lanes)
            lane = c * parts + part
            fy_rows_ref[pl.ds(SUB + lane, cells_y, stride=SUB), :] = fy_ref[:, cut]
            fy_rows_ref[pl.ds(lane, 1), :] = fy_halo_ref[0, SUB - 1 : SUB, cut]
            fy_rows_ref[pl.ds((cells_y + 1) * SUB + lane, 1), :] = fy_halo_ref[1, 0:1, cut]

    def candidate(n, carry):
        cell = list_ref[0, n]
        plane = cell // (cells_x * cells_y)
        row = cell // cells_y % cells_x
        column = cell % cells_y
        spot = (plane + 1) * per_plane + row + 1

        def at(ref, index):
            return ref[pl.ds(pl.multiple_of(index * SUB, SUB), SUB), :]

        centre = at(fy_rows_ref, column + 1)
        here = pl.ds(pl.multiple_of(n * SUB, SUB), SUB)
        prod_ref[0, here, :] = (at(rows_ref, spot + 1) - at(rows_ref, spot - 1)) * centre
        prod_ref[1, here, :] = at(rows_ref, spot) * (
            at(fy_rows_ref, column + 2) - at(fy_rows_ref, column)
        )
        prod_ref[2, here, :] = (
            at(rows_ref, spot + per_plane) - at(rows_ref, spot - per_plane)
        ) * centre
        return carry

    lax.fori_loop(0, count, candidate, 0, unroll=8)

    fh, fl = split(fy_ref[...])
    for c in range(comps):
        flat = jnp.concatenate(
            [
                wide_ref[y, c, 0:own, 0:cells_x, :].reshape(own * cells_x, ranks_b)
                for y in range(ny)
            ],
            axis=1,
        )
        high, low = split(flat)
        out = dot_last(high, fh) + dot_last(high, fl) + dot_last(low, fh)
        field_ref[c] = out.reshape(own, cells_x, cells_y)

    ones = jnp.ones((SUB * 2, lanes), F32).astype(BF16)

    def grad(c, d):
        total = prod_ref[d, pl.ds(c * parts, count, stride=SUB), :]
        for part in range(1, parts):
            total = total + prod_ref[d, pl.ds(c * parts + part, count, stride=SUB), :]
        high, low = split(total)
        return 0.5 * (dot_last(ones, high) + dot_last(ones, low))[0:1, :]

    j = [[grad(c, d) for d in range(3)] for c in range(3)]
    p = -(j[0][0] + j[1][1] + j[2][2])
    square = j[0][0] * j[0][0]
    for a in range(3):
        for b in range(3):
            if a + b > 0:
                square = square + j[a][b] * j[b][a]
    q = 0.5 * (p * p - square)
    det = (
        j[0][0] * (j[1][1] * j[2][2] - j[1][2] * j[2][1])
        - j[0][1] * (j[1][0] * j[2][2] - j[1][2] * j[2][0])
        + j[0][2] * (j[1][0] * j[2][1] - j[1][1] * j[2][0])
    )
    r = -det
    inv_ref[0:1, :] = p
    inv_ref[1:2, :] = q
    inv_ref[2:3, :] = r
    inv_ref[3:4, :] = q * q * q + 6.75 * r * r


def shards(sizes, core_tensor, factor_x, factor_y, factor_z, suspect_voxel_list):
    nx, ny, nz = sizes
    comps, ranks_z, ranks_a, ranks_b = core_tensor.shape
    planes = factor_z.shape[0]
    own = planes // nz
    chunk = own // HALVES
    cells_x, cells_y = factor_x.shape[0], factor_y.shape[0]
    ranks_x, ranks_y = factor_x.shape[1], factor_y.shape[1]
    rows = cells_x + SUB
    chunks = comps * HALVES
    count = suspect_voxel_list.shape[1]
    vmem = pl.BlockSpec(memory_space=pltpu.VMEM)
    dma = pltpu.SemaphoreType.DMA
    wide, fy_halo = pl.pallas_call(
        functools.partial(exchange_kernel, sizes),
        out_shape=(
            jax.ShapeDtypeStruct((ny, comps, own + 2, rows, ranks_b), F32),
            jax.ShapeDtypeStruct((2, SUB, ranks_y), F32),
        ),
        in_specs=[pl.BlockSpec(memory_space=pl.ANY)] * 4,
        out_specs=(vmem, vmem),
        scratch_shapes=[
            pltpu.VMEM((cells_x, ranks_x), F32),
            pltpu.VMEM((planes, ranks_z), F32),
            pltpu.VMEM((cells_x, ranks_x), F32),
            pltpu.VMEM((2 * (cells_x + 2 * SUB), ranks_x), BF16),
            pltpu.VMEM((chunks, chunk, rows, ranks_b), F32),
            dma((2,)),
            dma,
            dma,
            dma((chunks,)),
            dma((chunks,)),
            pltpu.VMEM((comps, ranks_z, ranks_a, ranks_b), F32),
            pltpu.VMEM((comps, planes, ranks_a, ranks_b), F32),
            pltpu.VMEM((comps, own, ranks_a, ranks_b), F32),
            pltpu.VMEM((chunks, nx, chunk, ranks_a, ranks_b), F32),
            pltpu.VMEM((2, SUB, ranks_x), F32),
            pltpu.VMEM((2 * planes * SUB, ranks_z * SUB), BF16),
            pltpu.VMEM((2 * (cells_x + 2 * SUB), ranks_x), BF16),
            dma((comps,)),
            dma((comps,)),
            dma((comps,)),
            dma((chunks, nx)),
            dma((chunks, nx)),
            dma((chunks, nx)),
            dma((chunks, max(ny - 1, 1))),
            dma((chunks, max(ny - 1, 1))),
            dma((comps, ny)),
            dma((comps, ny)),
            dma((2, 2)),
            dma((2, 2)),
        ],
        compiler_params=pltpu.CompilerParams(
            collective_id=0, has_side_effects=True, vmem_limit_bytes=52 * 2**20
        ),
    )(core_tensor, factor_x, factor_y, factor_z)
    field, invariants = pl.pallas_call(
        functools.partial(field_kernel, cells_x, cells_y),
        out_shape=(
            jax.ShapeDtypeStruct((comps, own, cells_x, cells_y), F32),
            jax.ShapeDtypeStruct((4, count), F32),
        ),
        in_specs=[vmem, vmem, vmem, pl.BlockSpec(memory_space=pltpu.SMEM)],
        out_specs=(vmem, vmem),
        scratch_shapes=[
            pltpu.VMEM(((own + 2) * (cells_x + 2) * SUB, 128), F32),
            pltpu.VMEM(((cells_y + 2) * SUB, 128), F32),
            pltpu.VMEM((3, count * SUB, 128), F32),
        ],
        compiler_params=pltpu.CompilerParams(vmem_limit_bytes=52 * 2**20),
    )(wide, factor_y, fy_halo, suspect_voxel_list)
    return field, invariants


def solution(mesh):
    placed = (
        P("grp", "gz", "gx", "gy"),
        P("gx", "grp"),
        P("gy", "grp"),
        P("grp", "gz"),
        P(("gx", "gy", "gz"), "grp"),
    )
    sizes = (mesh.shape["gx"], mesh.shape["gy"], mesh.shape["gz"])
    return jax.shard_map(
        functools.partial(shards, sizes),
        mesh=mesh,
        in_specs=placed,
        out_specs=(P("grp", "gz", "gx", "gy"), P("grp", ("gx", "gy", "gz"))),
        check_vma=False,
    )
```
